256 devices in a mesh: dp: 32 (over x, z), tensor: 8 (over y, core).
Axes of the slice: x: 4, y: 4, z: 8, core: 2. Of those that a mesh axis runs over, the one named last changes fastest.
Arguments:
- train_acts: bfloat16 [128, 256, 14336], P('dp', None, 'tensor'), may hold values from -16 to 16
- train_grads: bfloat16 [128, 256, 4096], P('dp', None, 'tensor'), may hold values from -16 to 16
- query_acts: bfloat16 [128, 256, 14336], P('dp', None, 'tensor'), may hold values from -16 to 16
- query_grads: bfloat16 [128, 256, 4096], P('dp', None, 'tensor'), may hold values from -16 to 16
- proj_in: bfloat16 [64, 14336], P(None, 'tensor'), may hold values from -0.046875 to 0.046875
- proj_out: bfloat16 [64, 4096], P(None, 'tensor'), may hold values from -0.09375 to 0.09375
Outputs:
- scores: float32 [128, 128], P('dp')
The draws below stay inside these ranges and needn't reach their ends.
All inputs are finite; a program needn't handle non-finite values.
Results may differ from the reference program's by a relative error of at most 0.0003.
Values sent between devices are 32-bit elements; how exact they have to be, the bound alone decides.
No kernel may reach another device: no remote copies, remote signals or barrier semaphores. Data moves between devices by JAX's collectives and lax.ppermute only.
A program may use at most 64 MiB of HBM per device.

```python
import jax
import jax.numpy as jnp
from jax import lax

D = 4096
HID = 14336
RANK = 64
SEQ = 256
TRAIN = 128
QUERY = 128


def shared_direction(key, width, salt):
    return jnp.clip(jax.random.normal(jax.random.fold_in(key, salt), (width,), jnp.float32), -4.0, 4.0)


def with_common(key, noise, direction):
    common = jnp.clip(jax.random.normal(key, noise.shape[:2] + (1,), jnp.float32), -4.0, 4.0) * 0.5
    return (noise + common * direction).astype(jnp.bfloat16)


def draw_train_acts(key, part):
    direction = shared_direction(key, HID, 100)
    key = jax.random.fold_in(key, 1)
    first, second = jax.random.split(key)
    noise = jnp.clip(jax.random.normal(first, (TRAIN, SEQ, HID), jnp.float32), -6.0, 6.0)
    return with_common(second, noise, direction)


def draw_train_grads(key, part):
    direction = shared_direction(key, D, 200)
    key = jax.random.fold_in(key, 2)
    first, second = jax.random.split(key)
    noise = jnp.clip(jax.random.normal(first, (TRAIN, SEQ, D), jnp.float32), -6.0, 6.0)
    return with_common(second, noise, direction)


def draw_query_acts(key, part):
    direction = shared_direction(key, HID, 100)
    key = jax.random.fold_in(key, 3)
    first, second = jax.random.split(key)
    noise = jnp.clip(jax.random.normal(first, (QUERY, SEQ, HID), jnp.float32), -6.0, 6.0)
    return with_common(second, noise, direction)


def draw_query_grads(key, part):
    direction = shared_direction(key, D, 200)
    key = jax.random.fold_in(key, 4)
    first, second = jax.random.split(key)
    noise = jnp.clip(jax.random.normal(first, (QUERY, SEQ, D), jnp.float32), -6.0, 6.0)
    return with_common(second, noise, direction)


def steps_of(stream_key, dims, shards, smallest, largest):
    level, own = 1.0, jax.random.fold_in(stream_key, 6)
    for dim, blocks in shards:
        heights = jnp.exp(jax.random.uniform(jax.random.fold_in(own, dim), (blocks,), jnp.float32, smallest / len(shards), largest / len(shards)))
        level = level * jnp.repeat(heights, dims[dim] // blocks).reshape([-1 if axis == dim else 1 for axis in range(len(dims))])
    return level


def bell_draw(rng, dims, spread, most, cuts=(), held_as=jnp.bfloat16):
    gain = steps_of(rng, dims, cuts, -0.22, 0.18) if cuts else 1.0
    drawn = jax.random.normal(rng, dims, jnp.float32) * spread * gain
    return jnp.minimum(jnp.maximum(drawn, -most), most).astype(held_as)


def setup_inputs(seed: int = 0) -> dict:
    keys = jax.random.split(jax.random.key(seed), 7)
    train_acts = draw_train_acts(jax.random.fold_in(keys[6], 71), 0)
    train_grads = draw_train_grads(jax.random.fold_in(keys[6], 71), 0)
    query_acts = draw_query_acts(jax.random.fold_in(keys[6], 71), 0)
    query_grads = draw_query_grads(jax.random.fold_in(keys[6], 71), 0)
    proj_in = bell_draw(keys[4], (RANK, HID), HID ** -0.5, 0.046875, ((1, 8),))
    proj_out = bell_draw(keys[5], (RANK, D), D ** -0.5, 0.09375, ((1, 8),))
    return dict(train_acts=train_acts, train_grads=train_grads, query_acts=query_acts, query_grads=query_grads, proj_in=proj_in, proj_out=proj_out)


damping = 0.1

def project(acts, grads, proj_in, proj_out):
    rows_in = acts.reshape(-1, acts.shape[-1])
    rows_out = grads.reshape(-1, grads.shape[-1])
    feat_in = lax.dot_general(rows_in.astype(jnp.float32), proj_in.astype(jnp.float32), (((1,), (1,)), ((), ())), preferred_element_type=jnp.float32)
    feat_out = lax.dot_general(rows_out.astype(jnp.float32), proj_out.astype(jnp.float32), (((1,), (1,)), ((), ())), preferred_element_type=jnp.float32)
    return (feat_in, feat_out)

def seq_grads(feat_in, feat_out, count):
    feat_in = feat_in.reshape(count, -1, feat_in.shape[-1])
    feat_out = feat_out.reshape(count, -1, feat_out.shape[-1])
    return jnp.einsum('sto,sti->soi', feat_out, feat_in, precision=lax.Precision.HIGHEST)

def precondition(grads, lower_in, lower_out):

    def single(grad):
        left = jax.scipy.linalg.cho_solve((lower_out, True), grad)
        return jax.scipy.linalg.cho_solve((lower_in, True), left.T).T
    return jax.vmap(single)(grads)

def reference(train_acts, train_grads, query_acts, query_grads, proj_in, proj_out):
    train_in, train_out = project(train_acts, train_grads, proj_in, proj_out)
    query_in, query_out = project(query_acts, query_grads, proj_in, proj_out)
    total = TRAIN * SEQ
    identity = jnp.eye(RANK, dtype=jnp.float32)
    factor_in = jnp.dot(train_in.T, train_in, precision=lax.Precision.HIGHEST) / total + damping * identity
    factor_out = jnp.dot(train_out.T, train_out, precision=lax.Precision.HIGHEST) / total + damping * identity
    train_grad = seq_grads(train_in, train_out, TRAIN)
    query_grad = seq_grads(query_in, query_out, QUERY)
    ready = precondition(query_grad, jnp.linalg.cholesky(factor_in), jnp.linalg.cholesky(factor_out))
    scores = jnp.einsum('toi,qoi->tq', train_grad, ready, precision=lax.Precision.HIGHEST)
    return scores / (SEQ * RANK)
```

```python
import functools

import jax
import jax.numpy as jnp
from jax import lax
from jax.experimental import pallas as pl
from jax.experimental.pallas import tpu as pltpu
from jax.sharding import Mesh
from jax.sharding import PartitionSpec as P

damping = 0.1
RANK = 64
LANES = 128
PANEL = 8
HIGH = lax.Precision.HIGHEST

VM = pl.BlockSpec(memory_space=pltpu.VMEM)
SM = pl.BlockSpec(memory_space=pltpu.SMEM)
PARAMS = pltpu.CompilerParams(vmem_limit_bytes=32 * 1024 * 1024)


def call(body, out, scratch=()):
    def wrapped(*args):
        return pl.pallas_call(
            body,
            out_shape=out,
            in_specs=[SM] + [VM] * (len(args) - 1),
            out_specs=jax.tree.map(lambda _: VM, out),
            scratch_shapes=list(scratch),
            compiler_params=PARAMS,
        )(*args)

    return wrapped


def f32(*shape):
    return jax.ShapeDtypeStruct(shape, jnp.float32)


def iota(shape, dim):
    return lax.broadcasted_iota(jnp.int32, shape, dim)


def pack(wide):
    lane = iota((32, LANES), 1)
    return jnp.where(lane < RANK, wide[:32], pltpu.roll(wide[32:], RANK, 1))


def unpack(packed):
    return jnp.concatenate([packed, pltpu.roll(packed, RANK, 1)], axis=0)


def gram_kernel(place, parts, send, own):
    total = (parts[0] + parts[1]) + (parts[2] + parts[3])
    gram = lax.dot_general(
        total, total, (((0,), (0,)), ((), ())), precision=HIGH, preferred_element_type=jnp.float32
    )
    top = gram[:RANK]
    low = gram[RANK:]
    side_out = pltpu.roll(low, RANK, 1)
    row = iota((RANK, LANES), 0)
    lane = iota((RANK, LANES), 1)
    both = pack(jnp.where(row <= lane, top, side_out))
    diag = jnp.sum(jnp.where(row == lane, side_out, 0.0), axis=0, keepdims=True)
    grad = pack(low)
    own[...] = grad
    is_train = place[3] == 0
    first = jnp.where(is_train, both, grad)
    rest = jnp.broadcast_to(diag, (8, LANES))
    for peer in range(send.shape[0]):
        send[peer, :32] = first
        send[peer, 32:40] = rest


def spread_kernel(place, got, own, send):
    @pl.when(place[3] == 0)
    def _():
        total = got[0]
        for peer in range(1, got.shape[0]):
            total = total + got[peer]
        grad = own[...]
        for peer in range(send.shape[0]):
            send[peer, :40] = total
            send[peer, 40:72] = grad

    @pl.when(place[3] != 0)
    def _():
        for share in range(4):
            for query in range(got.shape[0]):
                tile = got[query, 8 * share : 8 * share + 8]
                for column in range(4):
                    send[column * 4 + share, 8 * query : 8 * query + 8] = tile
        for peer in range(send.shape[0]):
            send[peer, 64:72] = got[0, 32:40]


def invert(wide):
    lane = iota((1, LANES), 1)
    sub = iota((RANK, 1), 0)
    left = lane < RANK
    inner = lane & (RANK - 1)
    for start in range(0, RANK, PANEL):
        columns = [
            jnp.where(
                left,
                jnp.broadcast_to(wide[:, k : k + 1], (RANK, LANES)),
                jnp.broadcast_to(wide[:, RANK + k : RANK + k + 1], (RANK, LANES)),
            )
            for k in range(start, start + PANEL)
        ]
        for step in range(PANEL):
            k = start + step
            column = columns[step]
            inverse = 1.0 / column[k : k + 1]
            here = inner == k
            scaled = jnp.where(here, inverse, wide[k : k + 1] * inverse)
            is_row = sub == k
            wide = jnp.where(is_row, scaled, jnp.where(here, 0.0, wide) - column * scaled)
            for later in range(step + 1, PANEL):
                ratio = columns[later][k : k + 1] * inverse
                columns[later] = jnp.where(is_row, ratio, columns[later] - column * ratio)
    return wide


def ready_kernel(total_tokens, place, got, out, held):
    total = got[0, :40]
    for peer in range(1, got.shape[0]):
        total = total + got[peer, :40]
    both = unpack(total[:32])[:, :RANK]
    flipped = both.T
    diag = total[32:33, :RANK]
    row = iota((RANK, RANK), 0)
    lane = iota((RANK, RANK), 1)
    factor_in = jnp.where(row <= lane, both, flipped)
    factor_out = jnp.where(row > lane, both, jnp.where(row == lane, diag, flipped))
    eye = jnp.where(row == lane, damping, 0.0)
    wide = jnp.concatenate(
        [factor_in * (1.0 / total_tokens) + eye, factor_out * (1.0 / total_tokens) + eye], axis=1
    )
    wide = invert(wide)
    held[...] = pltpu.roll(wide, RANK, 1)
    inverse_in = wide[:, :RANK]
    share = pl.multiple_of(place[2] * 8, 8)
    inverse_out = jnp.concatenate(
        [held[pl.ds(share, 8), :RANK], held[pl.ds(share + 32, 8), :RANK]], axis=0
    )
    lefts = []
    for seq in range(4):
        grad = unpack(got[place[0] * 4 + seq, 40:72])[:, :RANK]
        lefts.append(
            jnp.dot(inverse_out, grad, precision=HIGH, preferred_element_type=jnp.float32)
        )
    ready = jnp.dot(
        jnp.concatenate(lefts, axis=0), inverse_in, precision=HIGH, preferred_element_type=jnp.float32
    )
    ready = jnp.concatenate([ready, ready], axis=1)
    half = iota((8, LANES), 1) < RANK
    for seq in range(4):
        out[8 * seq : 8 * seq + 8] = jnp.where(
            half, ready[16 * seq : 16 * seq + 8], ready[16 * seq + 8 : 16 * seq + 16]
        )


def score_kernel(scale, place, got, ready, send):
    tiles = []
    for x in range(4):
        for z in range(8):
            for y in range(4):
                tiles.append(got[x * 4 + y, 8 * z : 8 * z + 8])
    queries = jnp.concatenate(tiles, axis=0)
    pairs = lax.dot_general(
        queries,
        ready[...],
        (((1,), (1,)), ((), ())),
        precision=HIGH,
        preferred_element_type=jnp.float32,
    )
    count = len(tiles)
    same = (iota((8 * count, 32), 0) & 7) == (iota((8 * count, 32), 1) & 7)
    sums = jnp.where(same, pairs, 0.0).reshape(count, 8, 32).sum(axis=1)
    pick = jnp.where(iota((8, 32), 0) == iota((8, 32), 1) // 8, scale, 0.0)
    scores = lax.dot_general(
        pick, sums, (((1,), (1,)), ((), ())), precision=HIGH, preferred_element_type=jnp.float32
    )
    for peer in range(send.shape[0]):
        send[peer] = scores


def total_kernel(place, got, out):
    total = (got[1] + got[3]) + (got[5] + got[7])
    out[...] = total[:4]


def features(acts, grads, proj_in, proj_out):
    rows_in = acts.reshape(-1, acts.shape[-1])
    rows_out = grads.reshape(-1, grads.shape[-1])
    feat_in = lax.dot_general(
        rows_in, proj_in, (((1,), (1,)), ((), ())), preferred_element_type=jnp.float32
    )
    feat_out = lax.dot_general(
        rows_out, proj_out, (((1,), (1,)), ((), ())), preferred_element_type=jnp.float32
    )
    return jnp.concatenate([feat_in, feat_out], axis=1)


def swap(value, axis):
    return lax.all_to_all(value, axis, 0, 0, tiled=True)


def on_device(train_acts, train_grads, query_acts, query_grads, proj_in, proj_out):
    seq_len = train_acts.shape[1]
    total_tokens = train_acts.shape[0] * seq_len * 32
    place = jnp.stack([lax.axis_index(name) for name in ("x", "z", "y", "c")]).astype(jnp.int32)
    is_train = place[3] == 0
    train = features(train_acts, train_grads, proj_in, proj_out)
    query = features(query_acts, query_grads, proj_in, proj_out)
    other = lax.ppermute(jnp.where(is_train, query, train), "c", [(0, 1), (1, 0)])
    mine = jnp.where(is_train, train, query) + other
    parts = swap(mine.reshape(4, seq_len, LANES), "y")
    send, own = call(gram_kernel, (f32(8, 40, LANES), f32(32, LANES)))(place, parts)
    got = swap(send, "z")
    send = call(spread_kernel, f32(16, 72, LANES))(place, got, own)
    got = swap(send, ("x", "y"))
    ready = call(
        functools.partial(ready_kernel, total_tokens),
        f32(32, LANES),
        [pltpu.VMEM((RANK, LANES), jnp.float32)],
    )(place, got)
    ready = lax.ppermute(ready, "c", [(0, 1), (1, 0)])
    scale = 1.0 / (seq_len * RANK)
    send = call(functools.partial(score_kernel, scale), f32(8, 8, LANES))(place, got, ready)
    return call(total_kernel, f32(4, LANES))(place, swap(send, ("y", "c")))


def solution(mesh):
    split = Mesh(mesh.devices.reshape(4, 8, 4, 2), ("x", "z", "y", "c"))
    dp = ("x", "z")
    tensor = ("y", "c")
    placed = (
        P(dp, None, tensor),
        P(dp, None, tensor),
        P(dp, None, tensor),
        P(dp, None, tensor),
        P(None, tensor),
        P(None, tensor),
    )
    return jax.shard_map(
        on_device, mesh=split, in_specs=placed, out_specs=P(dp, None), check_vma=False
    )
```

```python
import functools

import jax
import jax.numpy as jnp
from jax import lax
from jax.experimental import pallas as pl
from jax.experimental.pallas import tpu as pltpu
from jax.sharding import Mesh
from jax.sharding import PartitionSpec as P

damping = 0.1
RANK = 64
LANES = 128
HIGH = lax.Precision.HIGHEST

VM = pl.BlockSpec(memory_space=pltpu.VMEM)
SM = pl.BlockSpec(memory_space=pltpu.SMEM)
PARAMS = pltpu.CompilerParams(vmem_limit_bytes=32 * 1024 * 1024)


def call(body, out, scratch=()):
    def wrapped(*args):
        return pl.pallas_call(
            body,
            out_shape=out,
            in_specs=[SM] + [VM] * (len(args) - 1),
            out_specs=jax.tree.map(lambda _: VM, out),
            scratch_shapes=list(scratch),
            compiler_params=PARAMS,
        )(*args)

    return wrapped


def f32(*shape):
    return jax.ShapeDtypeStruct(shape, jnp.float32)


def iota(shape, dim):
    return lax.broadcasted_iota(jnp.int32, shape, dim)


def pack(wide):
    lane = iota((32, LANES), 1)
    return jnp.where(lane < RANK, wide[:32], pltpu.roll(wide[32:], RANK, 1))


def unpack(packed):
    return jnp.concatenate([packed, pltpu.roll(packed, RANK, 1)], axis=0)


def split(value):
    high = value.astype(jnp.bfloat16)
    return high, (value - high.astype(jnp.float32)).astype(jnp.bfloat16)


def gram_kernel(place, parts, send, own):
    total = (parts[0] + parts[1]) + (parts[2] + parts[3])
    terms = jnp.concatenate(split(total), axis=0)
    grams = lax.dot_general(
        terms, terms, (((1,), (1,)), ((), ())), preferred_element_type=jnp.float32
    )
    high, low = grams[:LANES], grams[LANES:]
    gram = high[:, :LANES] + ((high[:, LANES:] + low[:, :LANES]) + low[:, LANES:])
    top = gram[:RANK]
    low = gram[RANK:]
    side_out = pltpu.roll(low, RANK, 1)
    row = iota((RANK, LANES), 0)
    lane = iota((RANK, LANES), 1)
    both = pack(jnp.where(row <= lane, top, side_out))
    diag = jnp.sum(jnp.where(row == lane, side_out, 0.0), axis=0, keepdims=True)
    grad = pack(low)
    own[...] = grad
    is_train = place[3] == 0
    first = jnp.where(is_train, both, grad)
    rest = jnp.broadcast_to(diag, (8, LANES))
    for peer in range(send.shape[0]):
        send[peer, :32] = first
        send[peer, 32:40] = rest


def spread_kernel(place, got, own, send):
    @pl.when(place[3] == 0)
    def _():
        total = got[0]
        for peer in range(1, got.shape[0]):
            total = total + got[peer]
        grad = own[...]
        for peer in range(send.shape[0]):
            send[peer, :40] = total
            send[peer, 40:72] = grad

    @pl.when(place[3] != 0)
    def _():
        for share in range(4):
            for query in range(got.shape[0]):
                tile = got[query, 8 * share : 8 * share + 8]
                for column in range(4):
                    send[column * 4 + share, 8 * query : 8 * query + 8] = tile
        for peer in range(send.shape[0]):
            send[peer, 64:72] = got[0, 32:40]


def invert(wide):
    lane = iota((1, LANES), 1)
    sub = iota((8, 1), 0)
    left = lane < RANK
    inner = lane & (RANK - 1)
    blocks = [wide[8 * i : 8 * i + 8] for i in range(RANK // 8)]

    def spread(block, k):
        index = jnp.broadcast_to(jnp.where(left, k, RANK + k), (8, LANES))
        return jnp.take_along_axis(block, index, axis=1, mode="promise_in_bounds")

    def row_of(block, k):
        return jnp.broadcast_to(block[k : k + 1], (8, LANES))

    for at in range(RANK // 8):
        columns = [[spread(block, k) for block in blocks] for k in range(8 * at, 8 * at + 8)]
        for first in range(0, 8, 2):
            second = first + 1
            one, two = columns[first], columns[second]
            a, b = row_of(one[at], first), row_of(two[at], first)
            c, d = row_of(one[at], second), row_of(two[at], second)
            inverse = 1.0 / (a * d - b * c)

            def solve(upper, lower):
                return (d * upper - b * lower) * inverse, (a * lower - c * upper) * inverse

            is_first, is_second = sub == first, sub == second
            for later in range(second + 1, 8):
                column = columns[later]
                up, down = solve(row_of(column[at], first), row_of(column[at], second))
                column = [x - y * up - z * down for x, y, z in zip(column, one, two)]
                column[at] = jnp.where(is_first, up, jnp.where(is_second, down, column[at]))
                columns[later] = column
            here = inner == 8 * at + first
            there = inner == 8 * at + second
            rows = blocks[at]
            up, down = solve(row_of(rows, first), row_of(rows, second))
            up = jnp.where(here, d * inverse, jnp.where(there, -b * inverse, up))
            down = jnp.where(here, -c * inverse, jnp.where(there, a * inverse, down))
            both = here | there
            blocks = [
                jnp.where(both, 0.0, x) - y * up - z * down for x, y, z in zip(blocks, one, two)
            ]
            blocks[at] = jnp.where(is_first, up, jnp.where(is_second, down, blocks[at]))
    return jnp.concatenate(blocks, axis=0)


def ready_kernel(total_tokens, place, got, out, held):
    total = got[0, :40]
    for peer in range(1, got.shape[0]):
        total = total + got[peer, :40]
    both = unpack(total[:32])[:, :RANK]
    flipped = both.T
    diag = total[32:33, :RANK]
    row = iota((RANK, RANK), 0)
    lane = iota((RANK, RANK), 1)
    factor_in = jnp.where(row <= lane, both, flipped)
    factor_out = jnp.where(row > lane, both, jnp.where(row == lane, diag, flipped))
    eye = jnp.where(row == lane, damping, 0.0)
    wide = jnp.concatenate(
        [factor_in * (1.0 / total_tokens) + eye, factor_out * (1.0 / total_tokens) + eye], axis=1
    )
    wide = invert(wide)
    held[...] = pltpu.roll(wide, RANK, 1)
    inverse_in = wide[:, :RANK]
    share = pl.multiple_of(place[2] * 8, 8)
    inverse_out = jnp.concatenate([held[pl.ds(share, 8)], held[pl.ds(share + 32, 8)]], axis=0)
    halves = jnp.concatenate([inverse_out[:, :32], inverse_out[:, 32:RANK]], axis=0)
    grads = jnp.concatenate([got[place[0] * 4 + seq, 40:72] for seq in range(4)], axis=1)
    products = jnp.dot(halves, grads, precision=HIGH, preferred_element_type=jnp.float32)
    lefts = []
    for seq in range(4):
        product = products[:, LANES * seq : LANES * seq + LANES]
        lefts.append(product[:16] + pltpu.roll(product[16:], RANK, 1))
    ready = jnp.dot(
        jnp.concatenate(lefts, axis=0)[:, :RANK],
        inverse_in,
        precision=HIGH,
        preferred_element_type=jnp.float32,
    )
    ready = jnp.concatenate([ready, ready], axis=1)
    half = iota((8, LANES), 1) < RANK
    for seq in range(4):
        out[8 * seq : 8 * seq + 8] = jnp.where(
            half, ready[16 * seq : 16 * seq + 8], ready[16 * seq + 8 : 16 * seq + 16]
        )


def score_kernel(scale, place, got, ready, send):
    tiles = []
    for x in range(4):
        for z in range(8):
            for y in range(4):
                tiles.append(got[x * 4 + y, 8 * z : 8 * z + 8])
    queries = jnp.concatenate(tiles, axis=0)
    high, low = split(queries)
    both = jnp.concatenate(split(ready[...]), axis=0)
    dims = (((1,), (1,)), ((), ()))
    pairs = lax.dot_general(high, both, dims, preferred_element_type=jnp.float32)
    pairs += lax.dot_general(low, both, dims, preferred_element_type=jnp.float32)
    pairs = pairs[:, :32] + pairs[:, 32:]
    count = len(tiles)
    same = (iota((8 * count, 32), 0) & 7) == (iota((8 * count, 32), 1) & 7)
    sums = jnp.where(same, pairs, 0.0).reshape(count, 8, 32).sum(axis=1)
    pick = jnp.where(iota((8, 32), 0) == iota((8, 32), 1) // 8, scale, 0.0)
    scores = lax.dot_general(
        pick, sums, (((1,), (1,)), ((), ())), precision=HIGH, preferred_element_type=jnp.float32
    )
    for peer in range(send.shape[0]):
        send[peer] = scores


def features(acts, grads, proj_in, proj_out):
    dims = (((1,), (2,)), ((), ()))
    feat_in = lax.dot_general(proj_in, acts, dims, preferred_element_type=jnp.float32)
    feat_out = lax.dot_general(proj_out, grads, dims, preferred_element_type=jnp.float32)
    return jnp.concatenate([feat_in, feat_out], axis=0).transpose(1, 0, 2)


def swap(value, axis):
    return lax.all_to_all(value, axis, 0, 0, tiled=True)


def on_device(train_acts, train_grads, query_acts, query_grads, proj_in, proj_out):
    seq_len = train_acts.shape[1]
    total_tokens = train_acts.shape[0] * seq_len * 32
    place = jnp.stack([lax.axis_index(name) for name in ("x", "z", "y", "c")]).astype(jnp.int32)
    is_train = place[3] == 0
    train = features(train_acts, train_grads, proj_in, proj_out)
    query = features(query_acts, query_grads, proj_in, proj_out)
    other = lax.ppermute(jnp.where(is_train, query, train), "c", [(0, 1), (1, 0)])
    mine = jnp.where(is_train, train, query) + other
    place, mine = lax.optimization_barrier((place, mine))
    parts = swap(mine, "y")
    send, own = call(gram_kernel, (f32(8, 40, LANES), f32(32, LANES)))(place, parts)
    got = swap(send, "z")
    send = call(spread_kernel, f32(16, 72, LANES))(place, got, own)
    got = swap(send, ("x", "y"))
    queries = lax.ppermute(got, "c", [(0, 1), (1, 0)])
    ready = call(
        functools.partial(ready_kernel, total_tokens),
        f32(32, LANES),
        [pltpu.VMEM((RANK, LANES), jnp.float32)],
    )(place, got)
    scale = 1.0 / (seq_len * RANK)
    send = call(functools.partial(score_kernel, scale), f32(8, 8, LANES))(place, queries, ready)
    got = swap(send, ("y", "c"))
    return ((got[0] + got[2]) + (got[4] + got[6]))[:4]


def solution(mesh):
    split = Mesh(mesh.devices.reshape(4, 8, 4, 2), ("x", "z", "y", "c"))
    dp = ("x", "z")
    tensor = ("y", "c")
    placed = (
        P(dp, None, tensor),
        P(dp, None, tensor),
        P(dp, None, tensor),
        P(dp, None, tensor),
        P(None, tensor),
        P(None, tensor),
    )
    return jax.shard_map(
        on_device, mesh=split, in_specs=placed, out_specs=P(dp, None), check_vma=False
    )
```

```python
import functools

import jax
import jax.numpy as jnp
from jax import lax
from jax.experimental import pallas as pl
from jax.experimental.pallas import tpu as pltpu
from jax.sharding import Mesh
from jax.sharding import PartitionSpec as P

damping = 0.1
TRAIN_CORE = 1
RANK = 64
LANES = 128
HIGH = lax.Precision.HIGHEST

VM = pl.BlockSpec(memory_space=pltpu.VMEM)
PARAMS = pltpu.CompilerParams(vmem_limit_bytes=32 * 1024 * 1024)


def call(body, out, scratch=()):
    def wrapped(*args):
        return pl.pallas_call(
            body,
            out_shape=out,
            in_specs=[VM] * len(args),
            out_specs=jax.tree.map(lambda _: VM, out),
            scratch_shapes=list(scratch),
            compiler_params=PARAMS,
        )(*args)

    return wrapped


def f32(*shape):
    return jax.ShapeDtypeStruct(shape, jnp.float32)


def iota(shape, dim):
    return lax.broadcasted_iota(jnp.int32, shape, dim)


def pack(wide):
    lane = iota((32, LANES), 1)
    return jnp.where(lane < RANK, wide[:32], pltpu.roll(wide[32:], RANK, 1))


def unpack(packed):
    return jnp.concatenate([packed, pltpu.roll(packed, RANK, 1)], axis=0)


def split(value):
    high = value.astype(jnp.bfloat16)
    return high, (value - high.astype(jnp.float32)).astype(jnp.bfloat16)


def gram_kernel(parts, send, own):
    total = (parts[0] + parts[1]) + (parts[2] + parts[3])
    terms = jnp.concatenate(split(total), axis=0)
    grams = lax.dot_general(
        terms, terms, (((1,), (1,)), ((), ())), preferred_element_type=jnp.float32
    )
    high, low = grams[:LANES], grams[LANES:]
    gram = high[:, :LANES] + ((high[:, LANES:] + low[:, :LANES]) + low[:, LANES:])
    top = gram[:RANK]
    low = gram[RANK:]
    side_out = pltpu.roll(low, RANK, 1)
    row = iota((RANK, LANES), 0)
    lane = iota((RANK, LANES), 1)
    both = pack(jnp.where(row <= lane, top, side_out))
    diag = jnp.sum(jnp.where(row == lane, side_out, 0.0), axis=0, keepdims=True)
    grad = pack(low)
    own[...] = grad
    is_train = lax.axis_index("c") == TRAIN_CORE
    first = jnp.where(is_train, both, grad)
    rest = jnp.broadcast_to(diag, (8, LANES))
    for peer in range(send.shape[0]):
        send[peer, :32] = first
        send[peer, 32:40] = rest


def spread_kernel(got, own, send):
    @pl.when(lax.axis_index("c") == TRAIN_CORE)
    def _():
        total = got[0]
        for peer in range(1, got.shape[0]):
            total = total + got[peer]
        grad = own[...]
        for peer in range(send.shape[0]):
            send[peer, :40] = total
            send[peer, 40:72] = grad

    @pl.when(lax.axis_index("c") != TRAIN_CORE)
    def _():
        for share in range(4):
            for query in range(got.shape[0]):
                tile = got[query, 8 * share : 8 * share + 8]
                for column in range(4):
                    send[column * 4 + share, 8 * query : 8 * query + 8] = tile
        for peer in range(send.shape[0]):
            send[peer, 64:72] = got[0, 32:40]


def invert(wide):
    lane = iota((1, LANES), 1)
    sub = iota((8, 1), 0)
    left = lane < RANK
    inner = lane & (RANK - 1)
    blocks = [wide[8 * i : 8 * i + 8] for i in range(RANK // 8)]

    def spread(block, k):
        index = jnp.broadcast_to(jnp.where(left, k, RANK + k), (8, LANES))
        return jnp.take_along_axis(block, index, axis=1, mode="promise_in_bounds")

    def row_of(block, k):
        return jnp.broadcast_to(block[k : k + 1], (8, LANES))

    for at in range(RANK // 8):
        columns = [[spread(block, k) for block in blocks] for k in range(8 * at, 8 * at + 8)]
        for first in range(0, 8, 2):
            second = first + 1
            one, two = columns[first], columns[second]
            a, b = row_of(one[at], first), row_of(two[at], first)
            c, d = row_of(one[at], second), row_of(two[at], second)
            inverse = 1.0 / (a * d - b * c)

            def solve(upper, lower):
                return (d * upper - b * lower) * inverse, (a * lower - c * upper) * inverse

            is_first, is_second = sub == first, sub == second
            for later in range(second + 1, 8):
                column = columns[later]
                up, down = solve(row_of(column[at], first), row_of(column[at], second))
                column = [x - y * up - z * down for x, y, z in zip(column, one, two)]
                column[at] = jnp.where(is_first, up, jnp.where(is_second, down, column[at]))
                columns[later] = column
            here = inner == 8 * at + first
            there = inner == 8 * at + second
            rows = blocks[at]
            up, down = solve(row_of(rows, first), row_of(rows, second))
            up = jnp.where(here, d * inverse, jnp.where(there, -b * inverse, up))
            down = jnp.where(here, -c * inverse, jnp.where(there, a * inverse, down))
            both = here | there
            blocks = [
                jnp.where(both, 0.0, x) - y * up - z * down for x, y, z in zip(blocks, one, two)
            ]
            blocks[at] = jnp.where(is_first, up, jnp.where(is_second, down, blocks[at]))
    return jnp.concatenate(blocks, axis=0)


def ready_kernel(total_tokens, got, out, held):
    @pl.when(lax.axis_index("c") == TRAIN_CORE)
    def _():
        total = got[0, :40]
        for peer in range(1, got.shape[0]):
            total = total + got[peer, :40]
        both = unpack(total[:32])[:, :RANK]
        flipped = both.T
        diag = total[32:33, :RANK]
        row = iota((RANK, RANK), 0)
        lane = iota((RANK, RANK), 1)
        factor_in = jnp.where(row <= lane, both, flipped)
        factor_out = jnp.where(row > lane, both, jnp.where(row == lane, diag, flipped))
        eye = jnp.where(row == lane, damping, 0.0)
        wide = jnp.concatenate(
            [factor_in * (1.0 / total_tokens) + eye, factor_out * (1.0 / total_tokens) + eye], axis=1
        )
        wide = invert(wide)
        held[...] = pltpu.roll(wide, RANK, 1)
        inverse_in = wide[:, :RANK]
        share = pl.multiple_of(lax.axis_index("y") * 8, 8)
        inverse_out = jnp.concatenate([held[pl.ds(share, 8)], held[pl.ds(share + 32, 8)]], axis=0)
        halves = jnp.concatenate([inverse_out[:, :32], inverse_out[:, 32:RANK]], axis=0)
        grads = jnp.concatenate([got[lax.axis_index("x") * 4 + seq, 40:72] for seq in range(4)], axis=1)
        products = jnp.dot(halves, grads, precision=HIGH, preferred_element_type=jnp.float32)
        lefts = []
        for seq in range(4):
            product = products[:, LANES * seq : LANES * seq + LANES]
            lefts.append(product[:16] + pltpu.roll(product[16:], RANK, 1))
        ready = jnp.dot(
            jnp.concatenate(lefts, axis=0)[:, :RANK],
            inverse_in,
            precision=HIGH,
            preferred_element_type=jnp.float32,
        )
        ready = jnp.concatenate([ready, ready], axis=1)
        half = iota((8, LANES), 1) < RANK
        for seq in range(4):
            out[8 * seq : 8 * seq + 8] = jnp.where(
                half, ready[16 * seq : 16 * seq + 8], ready[16 * seq + 8 : 16 * seq + 16]
            )

    @pl.when(lax.axis_index("c") != TRAIN_CORE)
    def _():
        out[...] = jnp.zeros_like(out)


def score_kernel(scale, got, ready, send):
    tiles = []
    for x in range(4):
        for z in range(8):
            for y in range(4):
                tiles.append(got[x * 4 + y, 8 * z : 8 * z + 8])
    queries = jnp.concatenate(tiles, axis=0)
    high, low = split(queries)
    both = jnp.concatenate(split(ready[...]), axis=0)
    dims = (((1,), (1,)), ((), ()))
    pairs = lax.dot_general(high, both, dims, preferred_element_type=jnp.float32)
    pairs += lax.dot_general(low, both, dims, preferred_element_type=jnp.float32)
    pairs = pairs[:, :32] + pairs[:, 32:]
    count = len(tiles)
    same = (iota((8 * count, 32), 0) & 7) == (iota((8 * count, 32), 1) & 7)
    sums = jnp.where(same, pairs, 0.0).reshape(count, 8, 32).sum(axis=1)
    pick = jnp.where(iota((8, 32), 0) == iota((8, 32), 1) // 8, scale, 0.0)
    scores = lax.dot_general(
        pick, sums, (((1,), (1,)), ((), ())), precision=HIGH, preferred_element_type=jnp.float32
    )
    for peer in range(send.shape[0]):
        send[peer] = scores


def features(acts, grads, proj_in, proj_out):
    dims = (((1,), (2,)), ((), ()))
    feat_in = lax.dot_general(proj_in, acts, dims, preferred_element_type=jnp.float32)
    feat_out = lax.dot_general(proj_out, grads, dims, preferred_element_type=jnp.float32)
    return jnp.concatenate([feat_in, feat_out], axis=0).transpose(1, 0, 2)


def swap(value, axis):
    return lax.all_to_all(value, axis, 0, 0, tiled=True)


def on_device(train_acts, train_grads, query_acts, query_grads, proj_in, proj_out):
    seq_len = train_acts.shape[1]
    total_tokens = train_acts.shape[0] * seq_len * 32
    is_train = lax.axis_index("c") == TRAIN_CORE
    train = features(train_acts, train_grads, proj_in, proj_out)
    query = features(query_acts, query_grads, proj_in, proj_out)
    other = lax.ppermute(jnp.where(is_train, query, train), "c", [(0, 1), (1, 0)])
    mine = jnp.where(is_train, train, query) + other
    parts = swap(mine, "y")
    send, own = call(gram_kernel, (f32(8, 40, LANES), f32(32, LANES)))(parts)
    got = swap(send, "z")
    send = call(spread_kernel, f32(16, 72, LANES))(got, own)
    got = swap(send, ("x", "y"))
    ready = call(
        functools.partial(ready_kernel, total_tokens),
        f32(32, LANES),
        [pltpu.VMEM((RANK, LANES), jnp.float32)],
    )(got)
    ready = lax.ppermute(ready, "c", [(0, 1), (1, 0)])
    scale = 1.0 / (seq_len * RANK)
    send = call(functools.partial(score_kernel, scale), f32(8, 8, LANES))(got, ready)
    got = swap(send, ("y", "c"))
    return ((got[0] + got[2]) + (got[4] + got[6]))[:4]


def solution(mesh):
    split = Mesh(mesh.devices.reshape(4, 8, 4, 2), ("x", "z", "y", "c"))
    dp = ("x", "z")
    tensor = ("y", "c")
    placed = (
        P(dp, None, tensor),
        P(dp, None, tensor),
        P(dp, None, tensor),
        P(dp, None, tensor),
        P(None, tensor),
        P(None, tensor),
    )
    return jax.shard_map(
        on_device, mesh=split, in_specs=placed, out_specs=P(dp, None), check_vma=False
    )
```

```python
import functools

import jax
import jax.numpy as jnp
from jax import lax
from jax.experimental import pallas as pl
from jax.experimental.pallas import tpu as pltpu
from jax.sharding import Mesh
from jax.sharding import PartitionSpec as P

damping = 0.1
TRAIN_CORE = 1
RANK = 64
LANES = 128
HIGH = lax.Precision.HIGHEST

VM = pl.BlockSpec(memory_space=pltpu.VMEM)
PARAMS = pltpu.CompilerParams(vmem_limit_bytes=32 * 1024 * 1024)


def call(body, out, scratch=()):
    def wrapped(*args):
        return pl.pallas_call(
            body,
            out_shape=out,
            in_specs=[VM] * len(args),
            out_specs=jax.tree.map(lambda _: VM, out),
            scratch_shapes=list(scratch),
            compiler_params=PARAMS,
        )(*args)

    return wrapped


def f32(*shape):
    return jax.ShapeDtypeStruct(shape, jnp.float32)


def iota(shape, dim):
    return lax.broadcasted_iota(jnp.int32, shape, dim)


def pack(wide):
    lane = iota((32, LANES), 1)
    return jnp.where(lane < RANK, wide[:32], pltpu.roll(wide[32:], RANK, 1))


def unpack(packed):
    return jnp.concatenate([packed, pltpu.roll(packed, RANK, 1)], axis=0)


def split(value):
    high = value.astype(jnp.bfloat16)
    return high, (value - high.astype(jnp.float32)).astype(jnp.bfloat16)


def gram_kernel(parts, send, own):
    total = (parts[0] + parts[1]) + (parts[2] + parts[3])
    terms = jnp.concatenate(split(total), axis=0)
    grams = lax.dot_general(
        terms, terms, (((1,), (1,)), ((), ())), preferred_element_type=jnp.float32
    )
    high, low = grams[:LANES], grams[LANES:]
    gram = high[:, :LANES] + ((high[:, LANES:] + low[:, :LANES]) + low[:, LANES:])
    top = gram[:RANK]
    low = gram[RANK:]
    side_out = pltpu.roll(low, RANK, 1)
    row = iota((RANK, LANES), 0)
    lane = iota((RANK, LANES), 1)
    both = pack(jnp.where(row <= lane, top, side_out))
    diag = jnp.sum(jnp.where(row == lane, side_out, 0.0), axis=0, keepdims=True)
    grad = pack(low)
    own[...] = grad
    is_train = lax.axis_index("c") == TRAIN_CORE
    first = jnp.where(is_train, both, grad)
    rest = jnp.broadcast_to(diag, (8, LANES))
    for peer in range(send.shape[0]):
        send[peer, :32] = first
        send[peer, 32:40] = rest


def spread_kernel(got, own, send):
    @pl.when(lax.axis_index("c") == TRAIN_CORE)
    def _():
        total = got[0]
        for peer in range(1, got.shape[0]):
            total = total + got[peer]
        grad = own[...]
        for peer in range(send.shape[0]):
            send[peer, :40] = total
            send[peer, 40:72] = grad

    @pl.when(lax.axis_index("c") != TRAIN_CORE)
    def _():
        for share in range(4):
            for query in range(got.shape[0]):
                tile = got[query, 8 * share : 8 * share + 8]
                for column in range(4):
                    send[share * 4 + column, 8 * query : 8 * query + 8] = tile
        for peer in range(send.shape[0]):
            send[peer, 64:72] = got[0, 32:40]


def invert(wide):
    lane = iota((1, LANES), 1)
    sub = iota((8, 1), 0)
    left = lane < RANK
    inner = lane & (RANK - 1)
    blocks = [wide[8 * i : 8 * i + 8] for i in range(RANK // 8)]

    def spread(block, k):
        index = jnp.broadcast_to(jnp.where(left, k, RANK + k), (8, LANES))
        return jnp.take_along_axis(block, index, axis=1, mode="promise_in_bounds")

    def row_of(block, k):
        return jnp.broadcast_to(block[k : k + 1], (8, LANES))

    for at in range(RANK // 8):
        columns = [[spread(block, k) for block in blocks] for k in range(8 * at, 8 * at + 8)]
        for first in range(0, 8, 2):
            second = first + 1
            one, two = columns[first], columns[second]
            a, b = row_of(one[at], first), row_of(two[at], first)
            c, d = row_of(one[at], second), row_of(two[at], second)
            inverse = 1.0 / (a * d - b * c)

            def solve(upper, lower):
                return (d * upper - b * lower) * inverse, (a * lower - c * upper) * inverse

            is_first, is_second = sub == first, sub == second
            for later in range(second + 1, 8):
                column = columns[later]
                up, down = solve(row_of(column[at], first), row_of(column[at], second))
                column = [x - y * up - z * down for x, y, z in zip(column, one, two)]
                column[at] = jnp.where(is_first, up, jnp.where(is_second, down, column[at]))
                columns[later] = column
            here = inner == 8 * at + first
            there = inner == 8 * at + second
            rows = blocks[at]
            up, down = solve(row_of(rows, first), row_of(rows, second))
            up = jnp.where(here, d * inverse, jnp.where(there, -b * inverse, up))
            down = jnp.where(here, -c * inverse, jnp.where(there, a * inverse, down))
            both = here | there
            blocks = [
                jnp.where(both, 0.0, x) - y * up - z * down for x, y, z in zip(blocks, one, two)
            ]
            blocks[at] = jnp.where(is_first, up, jnp.where(is_second, down, blocks[at]))
    return jnp.concatenate(blocks, axis=0)


def ready_kernel(total_tokens, got, out, held):
    @pl.when(lax.axis_index("c") == TRAIN_CORE)
    def _():
        total = got[0, :40]
        for peer in range(1, got.shape[0]):
            total = total + got[peer, :40]
        both = unpack(total[:32])[:, :RANK]
        flipped = both.T
        diag = total[32:33, :RANK]
        row = iota((RANK, RANK), 0)
        lane = iota((RANK, RANK), 1)
        factor_in = jnp.where(row <= lane, both, flipped)
        factor_out = jnp.where(row > lane, both, jnp.where(row == lane, diag, flipped))
        eye = jnp.where(row == lane, damping, 0.0)
        wide = jnp.concatenate(
            [factor_in * (1.0 / total_tokens) + eye, factor_out * (1.0 / total_tokens) + eye], axis=1
        )
        wide = invert(wide)
        held[...] = pltpu.roll(wide, RANK, 1)
        inverse_in = wide[:, :RANK]
        share = pl.multiple_of(lax.axis_index("y") * 8, 8)
        inverse_out = jnp.concatenate([held[pl.ds(share, 8)], held[pl.ds(share + 32, 8)]], axis=0)
        halves = jnp.concatenate([inverse_out[:, :32], inverse_out[:, 32:RANK]], axis=0)
        grads = jnp.concatenate([got[seq * 4 + lax.axis_index("x"), 40:72] for seq in range(4)], axis=1)
        products = jnp.dot(halves, grads, precision=HIGH, preferred_element_type=jnp.float32)
        lefts = []
        for seq in range(4):
            product = products[:, LANES * seq : LANES * seq + LANES]
            lefts.append(product[:16] + pltpu.roll(product[16:], RANK, 1))
        ready = jnp.dot(
            jnp.concatenate(lefts, axis=0)[:, :RANK],
            inverse_in,
            precision=HIGH,
            preferred_element_type=jnp.float32,
        )
        ready = jnp.concatenate([ready, ready], axis=1)
        half = iota((8, LANES), 1) < RANK
        for seq in range(4):
            out[8 * seq : 8 * seq + 8] = jnp.where(
                half, ready[16 * seq : 16 * seq + 8], ready[16 * seq + 8 : 16 * seq + 16]
            )

    @pl.when(lax.axis_index("c") != TRAIN_CORE)
    def _():
        out[...] = jnp.zeros_like(out)


def split_kernel(got, out):
    @pl.when(lax.axis_index("c") != TRAIN_CORE)
    def _():
        for row in range(8):
            tiles = [got[peer, pl.ds(row, 8, stride=8), :] for peer in range(got.shape[0])]
            columns = slice(LANES * row, LANES * row + LANES)
            out[0, :, columns], out[1, :, columns] = split(jnp.concatenate(tiles, axis=0))


def score_kernel(scale, queries, ready, send):
    tiles = ready[...].reshape(4, 8, LANES)
    rows = [tiles[:, row, :] for row in range(8)]
    trains = jnp.concatenate(rows, axis=1)
    trains = jnp.concatenate([trains, trains], axis=0) * scale
    high, low = split(trains)
    high = high.astype(jnp.float32)
    terms = jnp.where(iota(trains.shape, 0) < 4, high, low.astype(jnp.float32))
    terms = terms.astype(jnp.bfloat16)
    dims = (((1,), (1,)), ((), ()))
    scores = lax.dot_general(terms, queries[0], dims, preferred_element_type=jnp.float32)
    scores += lax.dot_general(terms, queries[1], dims, preferred_element_type=jnp.float32)
    scores = scores + pltpu.roll(scores, 4, 0)
    lane = iota(scores.shape, 1)
    source = (lane & 3) * 32 + (lane >> 2)
    scores = jnp.take_along_axis(scores, source, axis=1, mode="promise_in_bounds")
    for peer in range(send.shape[0]):
        send[peer] = scores


def features(acts, grads, proj_in, proj_out):
    dims = (((1,), (2,)), ((), ()))
    feat_in = lax.dot_general(proj_in, acts, dims, preferred_element_type=jnp.float32)
    feat_out = lax.dot_general(proj_out, grads, dims, preferred_element_type=jnp.float32)
    return jnp.concatenate([feat_in, feat_out], axis=0).transpose(1, 0, 2)


def swap(value, axis):
    return lax.all_to_all(value, axis, 0, 0, tiled=True)


def on_device(train_acts, train_grads, query_acts, query_grads, proj_in, proj_out):
    seq_len = train_acts.shape[1]
    total_tokens = train_acts.shape[0] * seq_len * 32
    is_train = lax.axis_index("c") == TRAIN_CORE
    train = features(train_acts, train_grads, proj_in, proj_out)
    query = features(query_acts, query_grads, proj_in, proj_out)
    other = lax.ppermute(jnp.where(is_train, query, train), "c", [(0, 1), (1, 0)])
    mine = jnp.where(is_train, train, query) + other
    parts = swap(mine, "y")
    send, own = call(gram_kernel, (f32(8, 40, LANES), f32(32, LANES)))(parts)
    got = swap(send, "z")
    send = call(spread_kernel, f32(16, 72, LANES))(got, own)
    got = swap(send, ("y", "x"))
    ready = call(
        functools.partial(ready_kernel, total_tokens),
        f32(32, LANES),
        [pltpu.VMEM((RANK, LANES), jnp.float32)],
    )(got)
    ready = lax.ppermute(ready, "c", [(0, 1), (1, 0)])
    scale = 1.0 / (seq_len * RANK)
    queries = call(split_kernel, jax.ShapeDtypeStruct((2, LANES, 8 * LANES), jnp.bfloat16))(got)
    send = call(functools.partial(score_kernel, scale), f32(8, 8, LANES))(queries, ready)
    got = swap(send, ("c", "y"))
    return ((got[0] + got[1]) + (got[2] + got[3]))[:4]


def solution(mesh):
    split = Mesh(mesh.devices.reshape(4, 8, 4, 2), ("x", "z", "y", "c"))
    dp = ("x", "z")
    tensor = ("y", "c")
    placed = (
        P(dp, None, tensor),
        P(dp, None, tensor),
        P(dp, None, tensor),
        P(dp, None, tensor),
        P(None, tensor),
        P(None, tensor),
    )
    return jax.shard_map(
        on_device, mesh=split, in_specs=placed, out_specs=P(dp, None), check_vma=False
    )
```

```python
import functools

import jax
import jax.numpy as jnp
from jax import lax
from jax.experimental import pallas as pl
from jax.experimental.pallas import tpu as pltpu
from jax.sharding import Mesh
from jax.sharding import PartitionSpec as P

damping = 0.1
TRAIN_CORE = 1
RANK = 64
LANES = 128
HIGH = lax.Precision.HIGHEST

VM = pl.BlockSpec(memory_space=pltpu.VMEM)
PARAMS = pltpu.CompilerParams(vmem_limit_bytes=32 * 1024 * 1024)


def call(body, out, scratch=()):
    def wrapped(*args):
        return pl.pallas_call(
            body,
            out_shape=out,
            in_specs=[VM] * len(args),
            out_specs=jax.tree.map(lambda _: VM, out),
            scratch_shapes=list(scratch),
            compiler_params=PARAMS,
        )(*args)

    return wrapped


def f32(*shape):
    return jax.ShapeDtypeStruct(shape, jnp.float32)


def iota(shape, dim):
    return lax.broadcasted_iota(jnp.int32, shape, dim)


def pack(wide):
    lane = iota((32, LANES), 1)
    return jnp.where(lane < RANK, wide[:32], pltpu.roll(wide[32:], RANK, 1))


def unpack(packed):
    return jnp.concatenate([packed, pltpu.roll(packed, RANK, 1)], axis=0)


def split(value):
    terms = []
    for _ in range(3):
        term = value.astype(jnp.bfloat16)
        terms.append(term)
        value = value - term.astype(jnp.float32)
    return terms


def gram_kernel(parts, send, own):
    total = (parts[0] + parts[1]) + (parts[2] + parts[3])
    gram = lax.dot_general(
        total, total, (((1,), (1,)), ((), ())), precision=HIGH, preferred_element_type=jnp.float32
    )
    top = gram[:RANK]
    low = gram[RANK:]
    side_out = pltpu.roll(low, RANK, 1)
    row = iota((RANK, LANES), 0)
    lane = iota((RANK, LANES), 1)
    both = pack(jnp.where(row <= lane, top, side_out))
    diag = jnp.sum(jnp.where(row == lane, side_out, 0.0), axis=0, keepdims=True)
    grad = pack(low)
    own[...] = grad
    is_train = lax.axis_index("c") == TRAIN_CORE
    first = jnp.where(is_train, both, grad)
    rest = jnp.broadcast_to(diag, (8, LANES))
    for peer in range(send.shape[0]):
        send[peer, :32] = first
        send[peer, 32:40] = rest


def spread_kernel(got, own, send):
    @pl.when(lax.axis_index("c") == TRAIN_CORE)
    def _():
        total = got[0]
        for peer in range(1, got.shape[0]):
            total = total + got[peer]
        grad = own[...]
        for peer in range(send.shape[0]):
            send[peer, :40] = total
            send[peer, 40:72] = grad

    @pl.when(lax.axis_index("c") != TRAIN_CORE)
    def _():
        for share in range(4):
            for query in range(got.shape[0]):
                tile = got[query, 8 * share : 8 * share + 8]
                for column in range(4):
                    send[share * 4 + column, 8 * query : 8 * query + 8] = tile
        for peer in range(send.shape[0]):
            send[peer, 64:72] = got[0, 32:40]


def invert(wide):
    lane = iota((1, LANES), 1)
    sub = iota((8, 1), 0)
    left = lane < RANK
    inner = lane & (RANK - 1)
    blocks = [wide[8 * i : 8 * i + 8] for i in range(RANK // 8)]

    def spread(block, k):
        index = jnp.broadcast_to(jnp.where(left, k, RANK + k), (8, LANES))
        return jnp.take_along_axis(block, index, axis=1, mode="promise_in_bounds")

    def row_of(block, k):
        return jnp.broadcast_to(block[k : k + 1], (8, LANES))

    for at in range(RANK // 8):
        columns = [[spread(block, k) for block in blocks] for k in range(8 * at, 8 * at + 8)]
        for first in range(0, 8, 2):
            second = first + 1
            one, two = columns[first], columns[second]
            a, b = row_of(one[at], first), row_of(two[at], first)
            c, d = row_of(one[at], second), row_of(two[at], second)
            inverse = 1.0 / (a * d - b * c)

            def solve(upper, lower):
                return (d * upper - b * lower) * inverse, (a * lower - c * upper) * inverse

            is_first, is_second = sub == first, sub == second
            for later in range(second + 1, 8):
                column = columns[later]
                up, down = solve(row_of(column[at], first), row_of(column[at], second))
                column = [x - y * up - z * down for x, y, z in zip(column, one, two)]
                column[at] = jnp.where(is_first, up, jnp.where(is_second, down, column[at]))
                columns[later] = column
            here = inner == 8 * at + first
            there = inner == 8 * at + second
            rows = blocks[at]
            up, down = solve(row_of(rows, first), row_of(rows, second))
            up = jnp.where(here, d * inverse, jnp.where(there, -b * inverse, up))
            down = jnp.where(here, -c * inverse, jnp.where(there, a * inverse, down))
            both = here | there
            blocks = [
                jnp.where(both, 0.0, x) - y * up - z * down for x, y, z in zip(blocks, one, two)
            ]
            blocks[at] = jnp.where(is_first, up, jnp.where(is_second, down, blocks[at]))
    return jnp.concatenate(blocks, axis=0)


def ready_kernel(total_tokens, got, out, held):
    @pl.when(lax.axis_index("c") == TRAIN_CORE)
    def _():
        total = got[0, :40]
        for peer in range(1, got.shape[0]):
            total = total + got[peer, :40]
        both = unpack(total[:32])[:, :RANK]
        flipped = both.T
        diag = total[32:33, :RANK]
        row = iota((RANK, RANK), 0)
        lane = iota((RANK, RANK), 1)
        factor_in = jnp.where(row <= lane, both, flipped)
        factor_out = jnp.where(row > lane, both, jnp.where(row == lane, diag, flipped))
        eye = jnp.where(row == lane, damping, 0.0)
        wide = jnp.concatenate(
            [factor_in * (1.0 / total_tokens) + eye, factor_out * (1.0 / total_tokens) + eye], axis=1
        )
        wide = invert(wide)
        held[...] = pltpu.roll(wide, RANK, 1)
        inverse_in = wide[:, :RANK]
        share = pl.multiple_of(lax.axis_index("y") * 8, 8)
        inverse_out = jnp.concatenate([held[pl.ds(share, 8)], held[pl.ds(share + 32, 8)]], axis=0)
        halves = jnp.concatenate([inverse_out[:, :32], inverse_out[:, 32:RANK]], axis=0)
        grads = jnp.concatenate([got[seq * 4 + lax.axis_index("x"), 40:72] for seq in range(4)], axis=1)
        products = jnp.dot(halves, grads, precision=HIGH, preferred_element_type=jnp.float32)
        lefts = []
        for seq in range(4):
            product = products[:, LANES * seq : LANES * seq + LANES]
            lefts.append(product[:16] + pltpu.roll(product[16:], RANK, 1))
        ready = jnp.dot(
            jnp.concatenate(lefts, axis=0)[:, :RANK],
            inverse_in,
            precision=HIGH,
            preferred_element_type=jnp.float32,
        )
        ready = jnp.concatenate([ready, ready], axis=1)
        half = iota((8, LANES), 1) < RANK
        for seq in range(4):
            out[8 * seq : 8 * seq + 8] = jnp.where(
                half, ready[16 * seq : 16 * seq + 8], ready[16 * seq + 8 : 16 * seq + 16]
            )

    @pl.when(lax.axis_index("c") != TRAIN_CORE)
    def _():
        out[...] = jnp.zeros_like(out)


def split_kernel(got, out):
    @pl.when(lax.axis_index("c") != TRAIN_CORE)
    def _():
        for row in range(8):
            tiles = [got[peer, pl.ds(row, 8, stride=8), :] for peer in range(got.shape[0])]
            columns = slice(LANES * row, LANES * row + LANES)
            for index, term in enumerate(split(jnp.concatenate(tiles, axis=0))):
                out[index, :, columns] = term


def score_kernel(scale, queries, ready, send):
    tiles = ready[...].reshape(4, 8, LANES)
    rows = [tiles[:, row, :] for row in range(8)]
    trains = jnp.concatenate(rows, axis=1)
    trains = jnp.concatenate([trains] * 4, axis=0) * scale
    group = iota(trains.shape, 0) // 4
    terms = jnp.zeros_like(trains)
    for index, term in enumerate(split(trains)):
        terms = jnp.where(group == index, term.astype(jnp.float32), terms)
    terms = terms.astype(jnp.bfloat16)
    dims = (((1,), (1,)), ((), ()))
    scores = jnp.zeros((16, queries.shape[1]), jnp.float32)
    for index in range(queries.shape[0]):
        scores += lax.dot_general(terms, queries[index], dims, preferred_element_type=jnp.float32)
    scores = scores[:8] + scores[8:]
    scores = scores + pltpu.roll(scores, 4, 0)
    lane = iota(scores.shape, 1)
    source = (lane & 3) * 32 + (lane >> 2)
    scores = jnp.take_along_axis(scores, source, axis=1, mode="promise_in_bounds")
    for peer in range(send.shape[0]):
        send[peer] = scores


def features(acts, grads, proj_in, proj_out):
    dims = (((1,), (2,)), ((), ()))
    feat_in = lax.dot_general(proj_in, acts, dims, preferred_element_type=jnp.float32)
    feat_out = lax.dot_general(proj_out, grads, dims, preferred_element_type=jnp.float32)
    return jnp.concatenate([feat_in, feat_out], axis=0).transpose(1, 0, 2)


def swap(value, axis):
    return lax.all_to_all(value, axis, 0, 0, tiled=True)


def on_device(train_acts, train_grads, query_acts, query_grads, proj_in, proj_out):
    seq_len = train_acts.shape[1]
    total_tokens = train_acts.shape[0] * seq_len * 32
    is_train = lax.axis_index("c") == TRAIN_CORE
    train = features(train_acts, train_grads, proj_in, proj_out)
    query = features(query_acts, query_grads, proj_in, proj_out)
    other = lax.ppermute(jnp.where(is_train, query, train), "c", [(0, 1), (1, 0)])
    mine = jnp.where(is_train, train, query) + other
    parts = swap(mine, "y")
    send, own = call(gram_kernel, (f32(8, 40, LANES), f32(32, LANES)))(parts)
    got = swap(send, "z")
    send = call(spread_kernel, f32(16, 72, LANES))(got, own)
    got = swap(send, ("y", "x"))
    ready = call(
        functools.partial(ready_kernel, total_tokens),
        f32(32, LANES),
        [pltpu.VMEM((RANK, LANES), jnp.float32)],
    )(got)
    ready = lax.ppermute(ready, "c", [(0, 1), (1, 0)])
    scale = 1.0 / (seq_len * RANK)
    queries = call(split_kernel, jax.ShapeDtypeStruct((3, LANES, 8 * LANES), jnp.bfloat16))(got)
    send = call(functools.partial(score_kernel, scale), f32(8, 8, LANES))(queries, ready)
    got = swap(send, ("c", "y"))
    return ((got[0] + got[1]) + (got[2] + got[3]))[:4]


def solution(mesh):
    split = Mesh(mesh.devices.reshape(4, 8, 4, 2), ("x", "z", "y", "c"))
    dp = ("x", "z")
    tensor = ("y", "c")
    placed = (
        P(dp, None, tensor),
        P(dp, None, tensor),
        P(dp, None, tensor),
        P(dp, None, tensor),
        P(None, tensor),
        P(None, tensor),
    )
    return jax.shard_map(
        on_device, mesh=split, in_specs=placed, out_specs=P(dp, None), check_vma=False
    )
```

```python
import functools

import jax
import jax.numpy as jnp
from jax import lax
from jax.experimental import pallas as pl
from jax.experimental.pallas import tpu as pltpu
from jax.sharding import Mesh
from jax.sharding import PartitionSpec as P

damping = 0.1
TRAIN_CORE = 1
RANK = 64
LANES = 128
HIGH = lax.Precision.HIGHEST

VM = pl.BlockSpec(memory_space=pltpu.VMEM)
PARAMS = pltpu.CompilerParams(vmem_limit_bytes=32 * 1024 * 1024)


def call(body, out, scratch=()):
    def wrapped(*args):
        return pl.pallas_call(
            body,
            out_shape=out,
            in_specs=[VM] * len(args),
            out_specs=jax.tree.map(lambda _: VM, out),
            scratch_shapes=list(scratch),
            compiler_params=PARAMS,
        )(*args)

    return wrapped


def f32(*shape):
    return jax.ShapeDtypeStruct(shape, jnp.float32)


def iota(shape, dim):
    return lax.broadcasted_iota(jnp.int32, shape, dim)


def pack(wide):
    lane = iota((32, LANES), 1)
    return jnp.where(lane < RANK, wide[:32], pltpu.roll(wide[32:], RANK, 1))


def unpack(packed):
    return jnp.concatenate([packed, pltpu.roll(packed, RANK, 1)], axis=0)


def split(value):
    terms = []
    for _ in range(3):
        term = value.astype(jnp.bfloat16)
        terms.append(term)
        value = value - term.astype(jnp.float32)
    return terms


def gram_kernel(parts, send, own):
    total = (parts[0] + parts[1]) + (parts[2] + parts[3])
    dims = (((1,), (1,)), ((), ()))

    @pl.when(lax.axis_index("c") == TRAIN_CORE)
    def _():
        gram = lax.dot_general(
            total, total, dims, precision=HIGH, preferred_element_type=jnp.float32
        )
        low = gram[RANK:]
        side_out = pltpu.roll(low, RANK, 1)
        row = iota((RANK, LANES), 0)
        lane = iota((RANK, LANES), 1)
        both = pack(jnp.where(row <= lane, gram[:RANK], side_out))
        diag = jnp.sum(jnp.where(row == lane, side_out, 0.0), axis=0, keepdims=True)
        own[...] = pack(low)
        rest = jnp.broadcast_to(diag, (8, LANES))
        for peer in range(send.shape[0]):
            send[peer, :32] = both
            send[peer, 32:40] = rest

    @pl.when(lax.axis_index("c") != TRAIN_CORE)
    def _():
        low = lax.dot_general(
            total[RANK:], total, dims, precision=HIGH, preferred_element_type=jnp.float32
        )
        grad = pack(low)
        own[...] = grad
        for peer in range(send.shape[0]):
            send[peer, :32] = grad
            send[peer, 32:40] = grad[:8]


def spread_kernel(got, own, send):
    @pl.when(lax.axis_index("c") == TRAIN_CORE)
    def _():
        total = got[0]
        for peer in range(1, got.shape[0]):
            total = total + got[peer]
        grad = own[...]
        for peer in range(send.shape[0]):
            send[peer, :40] = total
            send[peer, 40:72] = grad

    @pl.when(lax.axis_index("c") != TRAIN_CORE)
    def _():
        for share in range(4):
            for query in range(got.shape[0]):
                tile = got[query, 8 * share : 8 * share + 8]
                for column in range(4):
                    send[share * 4 + column, 8 * query : 8 * query + 8] = tile
        for peer in range(send.shape[0]):
            send[peer, 64:72] = got[0, 32:40]


def invert(wide):
    lane = iota((1, LANES), 1)
    sub = iota((8, 1), 0)
    left = lane < RANK
    inner = lane & (RANK - 1)
    blocks = [wide[8 * i : 8 * i + 8] for i in range(RANK // 8)]

    def spread(block, k):
        index = jnp.broadcast_to(jnp.where(left, k, RANK + k), (8, LANES))
        return jnp.take_along_axis(block, index, axis=1, mode="promise_in_bounds")

    def row_of(block, k):
        return jnp.broadcast_to(block[k : k + 1], (8, LANES))

    for at in range(RANK // 8):
        columns = [[spread(block, k) for block in blocks] for k in range(8 * at, 8 * at + 8)]
        for first in range(0, 8, 2):
            second = first + 1
            one, two = columns[first], columns[second]
            a, b = row_of(one[at], first), row_of(two[at], first)
            c, d = row_of(one[at], second), row_of(two[at], second)
            inverse = 1.0 / (a * d - b * c)

            def solve(upper, lower):
                return (d * upper - b * lower) * inverse, (a * lower - c * upper) * inverse

            is_first, is_second = sub == first, sub == second
            for later in range(second + 1, 8):
                column = columns[later]
                up, down = solve(row_of(column[at], first), row_of(column[at], second))
                column = [x - y * up - z * down for x, y, z in zip(column, one, two)]
                column[at] = jnp.where(is_first, up, jnp.where(is_second, down, column[at]))
                columns[later] = column
            here = inner == 8 * at + first
            there = inner == 8 * at + second
            rows = blocks[at]
            up, down = solve(row_of(rows, first), row_of(rows, second))
            up = jnp.where(here, d * inverse, jnp.where(there, -b * inverse, up))
            down = jnp.where(here, -c * inverse, jnp.where(there, a * inverse, down))
            both = here | there
            blocks = [
                jnp.where(both, 0.0, x) - y * up - z * down for x, y, z in zip(blocks, one, two)
            ]
            blocks[at] = jnp.where(is_first, up, jnp.where(is_second, down, blocks[at]))
    return jnp.concatenate(blocks, axis=0)


def ready_kernel(total_tokens, got, out, held):
    @pl.when(lax.axis_index("c") == TRAIN_CORE)
    def _():
        total = got[0, :40]
        for peer in range(1, got.shape[0]):
            total = total + got[peer, :40]
        both = unpack(total[:32])[:, :RANK]
        flipped = both.T
        diag = total[32:33, :RANK]
        row = iota((RANK, RANK), 0)
        lane = iota((RANK, RANK), 1)
        factor_in = jnp.where(row <= lane, both, flipped)
        factor_out = jnp.where(row > lane, both, jnp.where(row == lane, diag, flipped))
        eye = jnp.where(row == lane, damping, 0.0)
        wide = jnp.concatenate(
            [factor_in * (1.0 / total_tokens) + eye, factor_out * (1.0 / total_tokens) + eye], axis=1
        )
        wide = invert(wide)
        held[...] = pltpu.roll(wide, RANK, 1)
        inverse_in = wide[:, :RANK]
        share = pl.multiple_of(lax.axis_index("y") * 8, 8)
        inverse_out = jnp.concatenate([held[pl.ds(share, 8)], held[pl.ds(share + 32, 8)]], axis=0)
        halves = jnp.concatenate([inverse_out[:, :32], inverse_out[:, 32:RANK]], axis=0)
        grads = jnp.concatenate([got[seq * 4 + lax.axis_index("x"), 40:72] for seq in range(4)], axis=1)
        products = jnp.dot(halves, grads, precision=HIGH, preferred_element_type=jnp.float32)
        lefts = []
        for seq in range(4):
            product = products[:, LANES * seq : LANES * seq + LANES]
            lefts.append(product[:16] + pltpu.roll(product[16:], RANK, 1))
        ready = jnp.dot(
            jnp.concatenate(lefts, axis=0)[:, :RANK],
            inverse_in,
            precision=HIGH,
            preferred_element_type=jnp.float32,
        )
        ready = jnp.concatenate([ready, ready], axis=1)
        half = iota((8, LANES), 1) < RANK
        for seq in range(4):
            out[8 * seq : 8 * seq + 8] = jnp.where(
                half, ready[16 * seq : 16 * seq + 8], ready[16 * seq + 8 : 16 * seq + 16]
            )

    @pl.when(lax.axis_index("c") != TRAIN_CORE)
    def _():
        out[...] = jnp.zeros_like(out)


def split_kernel(got, out):
    @pl.when(lax.axis_index("c") != TRAIN_CORE)
    def _():
        for row in range(8):
            tiles = [got[peer, pl.ds(row, 8, stride=8), :] for peer in range(got.shape[0])]
            columns = slice(LANES * row, LANES * row + LANES)
            for index, term in enumerate(split(jnp.concatenate(tiles, axis=0))):
                out[index, :, columns] = term


def score_kernel(scale, queries, ready, send):
    @pl.when(lax.axis_index("c") != TRAIN_CORE)
    def _():
        tiles = ready[...].reshape(4, 8, LANES)
        rows = [tiles[:, row, :] for row in range(8)]
        trains = jnp.concatenate(rows, axis=1)
        trains = jnp.concatenate([trains] * 4, axis=0) * scale
        group = iota(trains.shape, 0) // 4
        terms = jnp.zeros_like(trains)
        for index, term in enumerate(split(trains)):
            terms = jnp.where(group == index, term.astype(jnp.float32), terms)
        terms = terms.astype(jnp.bfloat16)
        dims = (((1,), (1,)), ((), ()))
        scores = jnp.zeros((16, queries.shape[1]), jnp.float32)
        for index in range(queries.shape[0]):
            scores += lax.dot_general(terms, queries[index], dims, preferred_element_type=jnp.float32)
        scores = scores[:8] + scores[8:]
        scores = scores + pltpu.roll(scores, 4, 0)
        lane = iota(scores.shape, 1)
        source = (lane & 3) * 32 + (lane >> 2)
        scores = jnp.take_along_axis(scores, source, axis=1, mode="promise_in_bounds")
        for peer in range(send.shape[0]):
            send[peer] = scores

    @pl.when(lax.axis_index("c") == TRAIN_CORE)
    def _():
        send[...] = jnp.zeros_like(send)


def product(weight, rows):
    return lax.dot_general(
        weight, rows, (((1,), (2,)), ((), ())), preferred_element_type=jnp.float32
    ).transpose(1, 0, 2)


def swap(value, axis):
    return lax.all_to_all(value, axis, 0, 0, tiled=True)


def on_device(train_acts, train_grads, query_acts, query_grads, proj_in, proj_out):
    seq_len = train_acts.shape[1]
    total_tokens = train_acts.shape[0] * seq_len * 32
    is_train = lax.axis_index("c") == TRAIN_CORE
    flip = [(0, 1), (1, 0)]
    train_in = product(proj_in, train_acts)
    query_in = product(proj_in, query_acts)
    other_in = jnp.where(is_train, query_in, train_in)
    proj_out, other_in = lax.optimization_barrier((proj_out, other_in))
    other_in = lax.ppermute(other_in, "c", flip)
    train_out = product(proj_out, train_grads)
    query_out = product(proj_out, query_grads)
    other_out = lax.ppermute(jnp.where(is_train, query_out, train_out), "c", flip)
    mine = jnp.where(
        is_train,
        jnp.concatenate([train_in, train_out], axis=1),
        jnp.concatenate([query_in, query_out], axis=1),
    ) + jnp.concatenate([other_in, other_out], axis=1)
    parts = swap(mine, "y")
    send, own = call(gram_kernel, (f32(8, 40, LANES), f32(32, LANES)))(parts)
    got = swap(send, "z")
    send = call(spread_kernel, f32(16, 72, LANES))(got, own)
    got = swap(send, ("y", "x"))
    ready = call(
        functools.partial(ready_kernel, total_tokens),
        f32(32, LANES),
        [pltpu.VMEM((RANK, LANES), jnp.float32)],
    )(got)
    ready = lax.ppermute(ready, "c", [(0, 1), (1, 0)])
    scale = 1.0 / (seq_len * RANK)
    queries = call(split_kernel, jax.ShapeDtypeStruct((3, LANES, 8 * LANES), jnp.bfloat16))(got)
    send = call(functools.partial(score_kernel, scale), f32(8, 8, LANES))(queries, ready)
    got = swap(send, ("c", "y"))
    return ((got[0] + got[1]) + (got[2] + got[3]))[:4]


def solution(mesh):
    split = Mesh(mesh.devices.reshape(4, 8, 4, 2), ("x", "z", "y", "c"))
    dp = ("x", "z")
    tensor = ("y", "c")
    placed = (
        P(dp, None, tensor),
        P(dp, None, tensor),
        P(dp, None, tensor),
        P(dp, None, tensor),
        P(None, tensor),
        P(None, tensor),
    )
    return jax.shard_map(
        on_device, mesh=split, in_specs=placed, out_specs=P(dp, None), check_vma=False
    )
```

```python
import functools

import jax
import jax.numpy as jnp
from jax import lax
from jax.experimental import pallas as pl
from jax.experimental.pallas import tpu as pltpu
from jax.sharding import Mesh
from jax.sharding import PartitionSpec as P

damping = 0.1
TRAIN_CORE = 1
RANK = 64
LANES = 128
HIGH = lax.Precision.HIGHEST

VM = pl.BlockSpec(memory_space=pltpu.VMEM)
PARAMS = pltpu.CompilerParams(vmem_limit_bytes=32 * 1024 * 1024)


def call(body, out, scratch=()):
    def wrapped(*args):
        return pl.pallas_call(
            body,
            out_shape=out,
            in_specs=[VM] * len(args),
            out_specs=jax.tree.map(lambda _: VM, out),
            scratch_shapes=list(scratch),
            compiler_params=PARAMS,
        )(*args)

    return wrapped


def f32(*shape):
    return jax.ShapeDtypeStruct(shape, jnp.float32)


def iota(shape, dim):
    return lax.broadcasted_iota(jnp.int32, shape, dim)


def pack(wide):
    lane = iota((32, LANES), 1)
    return jnp.where(lane < RANK, wide[:32], pltpu.roll(wide[32:], RANK, 1))


def unpack(packed):
    return jnp.concatenate([packed, pltpu.roll(packed, RANK, 1)], axis=0)


def split(value):
    terms = []
    for _ in range(3):
        term = value.astype(jnp.bfloat16)
        terms.append(term)
        value = value - term.astype(jnp.float32)
    return terms


def gram_kernel(parts, send, own):
    total = (parts[0] + parts[1]) + (parts[2] + parts[3])
    dims = (((1,), (1,)), ((), ()))

    @pl.when(lax.axis_index("c") == TRAIN_CORE)
    def _():
        gram = lax.dot_general(
            total, total, dims, precision=HIGH, preferred_element_type=jnp.float32
        )
        low = gram[RANK:]
        side_out = pltpu.roll(low, RANK, 1)
        row = iota((RANK, LANES), 0)
        lane = iota((RANK, LANES), 1)
        both = pack(jnp.where(row <= lane, gram[:RANK], side_out))
        diag = jnp.sum(jnp.where(row == lane, side_out, 0.0), axis=0, keepdims=True)
        own[...] = pack(low)
        rest = jnp.broadcast_to(diag, (8, LANES))
        for peer in range(send.shape[0]):
            for part in range(8):
                send[peer, part] = both[4 * part : 4 * part + 4]
            send[peer, 8] = rest[:4]

    @pl.when(lax.axis_index("c") != TRAIN_CORE)
    def _():
        low = lax.dot_general(
            total[RANK:], total, dims, precision=HIGH, preferred_element_type=jnp.float32
        )
        grad = pack(low)
        own[...] = grad
        for peer in range(send.shape[0]):
            for part in range(8):
                send[peer, part] = grad[4 * part : 4 * part + 4]
            send[peer, 8] = grad[:4]


def spread_kernel(got, own, send):
    @pl.when(lax.axis_index("c") == TRAIN_CORE)
    def _():
        total = got[0]
        for peer in range(1, got.shape[0]):
            total = total + got[peer]
        grad = own[...]
        total = jnp.concatenate([total[part] for part in range(9)] + [total[8]], axis=0)
        for peer in range(send.shape[0]):
            send[peer, :40] = total
            send[peer, 40:72] = grad

    @pl.when(lax.axis_index("c") != TRAIN_CORE)
    def _():
        for share in range(4):
            for query in range(got.shape[0]):
                tile = jnp.concatenate([got[query, 2 * share], got[query, 2 * share + 1]], axis=0)
                for column in range(4):
                    send[share * 4 + column, 8 * query : 8 * query + 8] = tile
        for peer in range(send.shape[0]):
            send[peer, 64:72] = tile


def invert(wide):
    lane = iota((1, LANES), 1)
    sub = iota((8, 1), 0)
    left = lane < RANK
    inner = lane & (RANK - 1)
    blocks = [wide[8 * i : 8 * i + 8] for i in range(RANK // 8)]

    def spread(block, k):
        index = jnp.broadcast_to(jnp.where(left, k, RANK + k), (8, LANES))
        return jnp.take_along_axis(block, index, axis=1, mode="promise_in_bounds")

    def row_of(block, k):
        return jnp.broadcast_to(block[k : k + 1], (8, LANES))

    for at in range(RANK // 8):
        columns = [[spread(block, k) for block in blocks] for k in range(8 * at, 8 * at + 8)]
        for first in range(0, 8, 2):
            second = first + 1
            one, two = columns[first], columns[second]
            a, b = row_of(one[at], first), row_of(two[at], first)
            c, d = row_of(one[at], second), row_of(two[at], second)
            inverse = 1.0 / (a * d - b * c)

            def solve(upper, lower):
                return (d * upper - b * lower) * inverse, (a * lower - c * upper) * inverse

            is_first, is_second = sub == first, sub == second
            for later in range(second + 1, 8):
                column = columns[later]
                up, down = solve(row_of(column[at], first), row_of(column[at], second))
                column = [x - y * up - z * down for x, y, z in zip(column, one, two)]
                column[at] = jnp.where(is_first, up, jnp.where(is_second, down, column[at]))
                columns[later] = column
            here = inner == 8 * at + first
            there = inner == 8 * at + second
            rows = blocks[at]
            up, down = solve(row_of(rows, first), row_of(rows, second))
            up = jnp.where(here, d * inverse, jnp.where(there, -b * inverse, up))
            down = jnp.where(here, -c * inverse, jnp.where(there, a * inverse, down))
            both = here | there
            blocks = [
                jnp.where(both, 0.0, x) - y * up - z * down for x, y, z in zip(blocks, one, two)
            ]
            blocks[at] = jnp.where(is_first, up, jnp.where(is_second, down, blocks[at]))
    return jnp.concatenate(blocks, axis=0)


def ready_kernel(total_tokens, got, out, held):
    @pl.when(lax.axis_index("c") == TRAIN_CORE)
    def _():
        total = got[0, :40]
        for peer in range(1, got.shape[0]):
            total = total + got[peer, :40]
        both = unpack(total[:32])[:, :RANK]
        flipped = both.T
        diag = total[32:33, :RANK]
        row = iota((RANK, RANK), 0)
        lane = iota((RANK, RANK), 1)
        factor_in = jnp.where(row <= lane, both, flipped)
        factor_out = jnp.where(row > lane, both, jnp.where(row == lane, diag, flipped))
        eye = jnp.where(row == lane, damping, 0.0)
        wide = jnp.concatenate(
            [factor_in * (1.0 / total_tokens) + eye, factor_out * (1.0 / total_tokens) + eye], axis=1
        )
        wide = invert(wide)
        held[...] = pltpu.roll(wide, RANK, 1)
        inverse_in = wide[:, :RANK]
        share = pl.multiple_of(lax.axis_index("y") * 8, 8)
        inverse_out = jnp.concatenate([held[pl.ds(share, 8)], held[pl.ds(share + 32, 8)]], axis=0)
        halves = jnp.concatenate([inverse_out[:, :32], inverse_out[:, 32:RANK]], axis=0)
        grads = jnp.concatenate([got[seq * 4 + lax.axis_index("x"), 40:72] for seq in range(4)], axis=1)
        products = jnp.dot(halves, grads, precision=HIGH, preferred_element_type=jnp.float32)
        lefts = []
        for seq in range(4):
            product = products[:, LANES * seq : LANES * seq + LANES]
            lefts.append(product[:16] + pltpu.roll(product[16:], RANK, 1))
        ready = jnp.dot(
            jnp.concatenate(lefts, axis=0)[:, :RANK],
            inverse_in,
            precision=HIGH,
            preferred_element_type=jnp.float32,
        )
        ready = jnp.concatenate([ready, ready], axis=1)
        half = iota((8, LANES), 1) < RANK
        for seq in range(4):
            out[8 * seq : 8 * seq + 8] = jnp.where(
                half, ready[16 * seq : 16 * seq + 8], ready[16 * seq + 8 : 16 * seq + 16]
            )

    @pl.when(lax.axis_index("c") != TRAIN_CORE)
    def _():
        out[...] = jnp.zeros_like(out)


def split_kernel(got, out):
    @pl.when(lax.axis_index("c") != TRAIN_CORE)
    def _():
        for row in range(8):
            tiles = [got[peer, pl.ds(row, 8, stride=8), :] for peer in range(got.shape[0])]
            columns = slice(LANES * row, LANES * row + LANES)
            for index, term in enumerate(split(jnp.concatenate(tiles, axis=0))):
                out[index, :, columns] = term


def score_kernel(scale, queries, ready, send):
    @pl.when(lax.axis_index("c") != TRAIN_CORE)
    def _():
        tiles = ready[...].reshape(4, 8, LANES)
        rows = [tiles[:, row, :] for row in range(8)]
        trains = jnp.concatenate(rows, axis=1)
        trains = jnp.concatenate([trains] * 4, axis=0) * scale
        group = iota(trains.shape, 0) // 4
        terms = jnp.zeros_like(trains)
        for index, term in enumerate(split(trains)):
            terms = jnp.where(group == index, term.astype(jnp.float32), terms)
        terms = terms.astype(jnp.bfloat16)
        dims = (((1,), (1,)), ((), ()))
        scores = jnp.zeros((16, queries.shape[1]), jnp.float32)
        for index in range(queries.shape[0]):
            scores += lax.dot_general(terms, queries[index], dims, preferred_element_type=jnp.float32)
        scores = scores[:8] + scores[8:]
        scores = scores + pltpu.roll(scores, 4, 0)
        lane = iota(scores.shape, 1)
        source = (lane & 3) * 32 + (lane >> 2)
        scores = jnp.take_along_axis(scores, source, axis=1, mode="promise_in_bounds")
        for peer in range(send.shape[0]):
            send[peer] = scores

    @pl.when(lax.axis_index("c") == TRAIN_CORE)
    def _():
        send[...] = jnp.zeros_like(send)


def product(weight, rows):
    return lax.dot_general(
        weight, rows, (((1,), (2,)), ((), ())), preferred_element_type=jnp.float32
    ).transpose(1, 0, 2)


def swap(value, axis):
    return lax.all_to_all(value, axis, 0, 0, tiled=True)


def on_device(train_acts, train_grads, query_acts, query_grads, proj_in, proj_out):
    seq_len = train_acts.shape[1]
    total_tokens = train_acts.shape[0] * seq_len * 32
    is_train = lax.axis_index("c") == TRAIN_CORE
    flip = [(0, 1), (1, 0)]
    train_in = product(proj_in, train_acts)
    query_in = product(proj_in, query_acts)
    other_in = jnp.where(is_train, query_in, train_in)
    proj_out, other_in = lax.optimization_barrier((proj_out, other_in))
    other_in = lax.ppermute(other_in, "c", flip)
    train_out = product(proj_out, train_grads)
    query_out = product(proj_out, query_grads)
    other_out = lax.ppermute(jnp.where(is_train, query_out, train_out), "c", flip)
    mine = jnp.where(
        is_train,
        jnp.concatenate([train_in, train_out], axis=1),
        jnp.concatenate([query_in, query_out], axis=1),
    ) + jnp.concatenate([other_in, other_out], axis=1)
    parts = swap(mine, "y")
    send, own = call(gram_kernel, (f32(8, 9, 4, LANES), f32(32, LANES)))(parts)
    got = swap(send, "z")
    send = call(spread_kernel, f32(16, 72, LANES))(got, own)
    got = swap(send, ("y", "x"))
    ready = call(
        functools.partial(ready_kernel, total_tokens),
        f32(32, LANES),
        [pltpu.VMEM((RANK, LANES), jnp.float32)],
    )(got)
    ready = lax.ppermute(ready, "c", [(0, 1), (1, 0)])
    scale = 1.0 / (seq_len * RANK)
    queries = call(split_kernel, jax.ShapeDtypeStruct((3, LANES, 8 * LANES), jnp.bfloat16))(got)
    send = call(functools.partial(score_kernel, scale), f32(8, 8, LANES))(queries, ready)
    got = swap(send, ("c", "y"))
    return ((got[0] + got[1]) + (got[2] + got[3]))[:4]


def solution(mesh):
    split = Mesh(mesh.devices.reshape(4, 8, 4, 2), ("x", "z", "y", "c"))
    dp = ("x", "z")
    tensor = ("y", "c")
    placed = (
        P(dp, None, tensor),
        P(dp, None, tensor),
        P(dp, None, tensor),
        P(dp, None, tensor),
        P(None, tensor),
        P(None, tensor),
    )
    return jax.shard_map(
        on_device, mesh=split, in_specs=placed, out_specs=P(dp, None), check_vma=False
    )
```
